32 devices in a mesh: dp: 4 (over z), ctx: 8 (over y, x, core).
Axes of the slice: x: 2, y: 2, z: 4, core: 2. Of those that a mesh axis runs over, the one named last changes fastest.
Arguments:
- hidden_in: bfloat16 [4, 1024, 768], P('dp', 'ctx'), may hold values from -6 to 6
- segment_ids: int32 [4, 1024], P('dp', 'ctx'), may hold values from 0 to 4, as said below
- w_qkv: bfloat16 [768, 2304], P('dp'), may hold values from -0.21875 to 0.21875
- w_out: bfloat16 [768, 768], P('dp'), may hold values from -4 to 4
- w_in: bfloat16 [768, 2304], P('dp'), may hold values from -0.21875 to 0.21875
- w_down: bfloat16 [1152, 768], P('dp'), may hold values from -0.1875 to 0.1875
- gain_attn: bfloat16 [768], P('dp'), may hold values from 0.5 to 1.5
- gain_mlp: bfloat16 [768], P('dp'), may hold values from 0.5 to 1.5
- cotangent: bfloat16 [4, 1024, 768], P('dp', 'ctx'), may hold values from -6 to 6
Outputs:
- output: bfloat16 [4, 1024, 768], P('dp', 'ctx')
- grad_input: float32 [4, 1024, 768], P('dp', 'ctx')
- grad_qkv: float32 [768, 2304], P('dp')
- grad_out: float32 [768, 768], P('dp')
- grad_in: float32 [768, 2304], P('dp')
- grad_down: float32 [1152, 768], P('dp')
- grad_gain_attn: float32 [768], P('dp')
- grad_gain_mlp: float32 [768], P('dp')
The draws below stay inside these ranges and needn't reach their ends.
Inputs may be any that keep to these rules, and one draw needn't show every extreme that they name: `segment_ids`: ids never fall along a sequence; each sequence holds documents 0 to 4; document 2 begins within the first 128 tokens and ends within the last 128; every other document is shorter than 128 tokens.
All inputs are finite; a program needn't handle non-finite values.
Results may differ from the reference program's by a relative error of at most 0.024.
Values may be sent and summed in bfloat16 or wider, within the bound.
A program may use at most 256 MiB of HBM per device.

```python
import math
import jax
import jax.numpy as jnp
from jax import lax

D = 768
HEADS = 12
HEAD_DIM = 64
FF = 1152
TOK_CTX = 128
SEQ = 1024
SEQS = 4


def draw_segment_ids(key, part):
    key = jax.random.fold_in(key, 11)
    splits = jax.random.split(key, 4)
    half_size = TOK_CTX // 2
    first_cut = jax.random.randint(splits[0], (SEQS, 1), 1, half_size)
    second_cut = jax.random.randint(splits[1], (SEQS, 1), half_size, TOK_CTX)
    third_cut = SEQ - TOK_CTX + jax.random.randint(splits[2], (SEQS, 1), 1, half_size)
    fourth_cut = third_cut + jax.random.randint(splits[3], (SEQS, 1), 1, half_size)
    position = jnp.arange(SEQ, dtype=jnp.int32)[None, :]
    document = (position >= first_cut).astype(jnp.int32) + (position >= second_cut).astype(jnp.int32)
    document = document + (position >= third_cut).astype(jnp.int32) + (position >= fourth_cut).astype(jnp.int32)
    return document.astype(jnp.int32)


def block_scale(rng, extent, cuts, low, top_value):
    gain = 1.0
    for dim, shards_of in cuts:
        draws = jax.random.uniform(jax.random.fold_in(jax.random.fold_in(rng, 6), dim), (shards_of,), jnp.float32, low / len(cuts), top_value / len(cuts))
        gain = gain * jnp.repeat(jnp.exp(draws), extent[dim] // shards_of).reshape((-1,) + (1,) * (len(extent) - 1 - dim))
    return gain


def bell_draw(own_key, extent, width, limit, cuts=(), kind=jnp.bfloat16):
    factor_of = block_scale(own_key, extent, cuts, -0.22, 0.18) if cuts else 1.0
    array = jax.random.normal(own_key, extent, jnp.float32) * width * factor_of
    return jnp.minimum(jnp.maximum(array, -limit), limit).astype(kind)


def setup_inputs(seed: int = 0) -> dict:
    key_list = jax.random.split(jax.random.key(seed), 10)
    hidden_in = bell_draw(key_list[0], (SEQS, SEQ, D), 1.0, 6.0, ((0, 4), (1, 8)))
    segment_ids = draw_segment_ids(jax.random.fold_in(key_list[9], 71), 0)
    w_qkv = bell_draw(key_list[2], (D, 3 * D), D ** -0.5, 0.21875, ((0, 4),))
    w_out = bell_draw(key_list[3], (D, D), (max(1, 3 * D // SEQ)) ** -0.5, 4.0, ((0, 4),))
    w_in = bell_draw(key_list[4], (D, 2 * FF), D ** -0.5, 0.21875, ((0, 4),))
    w_down = bell_draw(key_list[5], (FF, D), FF ** -0.5, 0.1875, ((0, 4),))
    gain_attn = jnp.clip(1.0 + 0.1 * jax.random.normal(key_list[6], (D,), jnp.float32), 0.5, 1.5).astype(jnp.bfloat16)
    gain_mlp = jnp.clip(1.0 + 0.1 * jax.random.normal(key_list[7], (D,), jnp.float32), 0.5, 1.5).astype(jnp.bfloat16)
    cotangent = bell_draw(key_list[8], (SEQS, SEQ, D), 1.0, 6.0, ((0, 4), (1, 8)))
    return dict(hidden_in=hidden_in, segment_ids=segment_ids, w_qkv=w_qkv, w_out=w_out, w_in=w_in, w_down=w_down, gain_attn=gain_attn, gain_mlp=gain_mlp, cotangent=cotangent)


EPSILON = 1e-05
ROPE_THETA = 160000.0
NEGATIVE = -1e+30
HIGHEST_PRECISION = lax.Precision.HIGHEST

@jax.custom_vjp
def low(v):
    return lax.optimization_barrier(v.astype(jnp.bfloat16)).astype(jnp.float32)

@jax.custom_vjp
def low_back(v):
    return v

def low_keep(v):
    return (low(v), None)

def low_pass(kept, grad):
    return (grad,)

def back_keep(v):
    return (v, None)

def back_low(kept, grad):
    return (low(grad),)
low.defvjp(low_keep, low_pass)
low_back.defvjp(back_keep, back_low)

def layer_norm(values, gain_row):
    average = lax.optimization_barrier(jnp.mean(values, axis=-1, keepdims=True))
    centred = values - average
    spread = lax.optimization_barrier(jnp.mean(centred * centred, axis=-1, keepdims=True))
    return centred * lax.rsqrt(spread + EPSILON) * gain_row

def rope_tables(first_row, row_count, head_size):
    position = (first_row + jnp.arange(row_count, dtype=jnp.int32)).astype(jnp.float32)
    frequency = ROPE_THETA ** (-jnp.arange(0, head_size, 2, dtype=jnp.float32) / head_size)
    angles = position[:, None] * frequency[None, :]
    angles = jnp.concatenate([angles, angles], axis=-1)
    return (jnp.cos(angles)[:, None, :], jnp.sin(angles)[:, None, :])

def rotary(values, cosines, sines):
    half_size = values.shape[-1] // 2
    turned = jnp.concatenate([-values[..., half_size:], values[..., :half_size]], axis=-1)
    return values * cosines + turned * sines

def geglu(gate_in, gate_up):
    return jax.nn.gelu(gate_in, approximate=False) * gate_up

def attend(queries, own_keys, own_values, id_row):
    block_rows = math.gcd(SEQ, 512)
    block_count = SEQ // block_rows
    score_scale = HEAD_DIM ** (-0.5)

    def one_block(pair):
        query_block, id_block = pair
        scores = jnp.einsum('qhe,khe->hqk', query_block, own_keys, precision=HIGHEST_PRECISION) * score_scale
        allowed = (id_block[:, None] == id_row[None, :])[None]
        scores = low_back(jnp.where(allowed, scores, NEGATIVE))
        highest = lax.optimization_barrier(jnp.max(scores, axis=-1, keepdims=True))
        weights = jnp.where(allowed, jnp.exp(scores - highest), 0.0)
        probabilities = low(weights / lax.optimization_barrier(jnp.sum(weights, axis=-1, keepdims=True)))
        return jnp.einsum('hqk,khe->qhe', probabilities, own_values, precision=HIGHEST_PRECISION)
    blocks = lax.map(jax.checkpoint(one_block), (queries.reshape(block_count, block_rows, HEADS, HEAD_DIM), id_row.reshape(block_count, block_rows)))
    return blocks.reshape(SEQ, HEADS, HEAD_DIM)

def sequence(tokens_in, id_row, w_qkv, w_out, w_in, w_down, gain_attn, gain_mlp, cosines, sines):
    normed_one = low(layer_norm(tokens_in, gain_attn))
    projected = low_back(jnp.dot(normed_one, w_qkv, precision=HIGHEST_PRECISION))
    head_shape = (SEQ, HEADS, HEAD_DIM)
    queries = low(rotary(projected[:, :D].reshape(head_shape), cosines, sines))
    own_keys = low(rotary(projected[:, D:2 * D].reshape(head_shape), cosines, sines))
    own_values = low(projected[:, 2 * D:].reshape(head_shape))
    attended = attend(queries, own_keys, own_values, id_row).reshape(SEQ, D)
    attended = low_back(low(attended))
    branch = low_back(jnp.dot(attended, w_out, precision=HIGHEST_PRECISION))
    middle = tokens_in + branch
    normed_two = low(layer_norm(middle, gain_mlp))
    lifted = low_back(jnp.dot(normed_two, w_in, precision=HIGHEST_PRECISION))
    mixed_units = low(geglu(lifted[:, :FF], lifted[:, FF:]))
    return middle + low_back(jnp.dot(mixed_units, w_down, precision=HIGHEST_PRECISION))

def reference(hidden_in, segment_ids, w_qkv, w_out, w_in, w_down, gain_attn, gain_mlp, cotangent):
    cosines, sines = rope_tables(0, SEQ, HEAD_DIM)

    def forward(tokens_all, w_qkv, w_out, w_in, w_down, gain_attn, gain_mlp):

        def one_sequence(pair):
            return sequence(pair[0], pair[1], w_qkv, w_out, w_in, w_down, gain_attn, gain_mlp, cosines, sines)
        return lax.map(one_sequence, (tokens_all, segment_ids))
    primals = (hidden_in.astype(jnp.float32), w_qkv.astype(jnp.float32), w_out.astype(jnp.float32), w_in.astype(jnp.float32), w_down.astype(jnp.float32), gain_attn.astype(jnp.float32), gain_mlp.astype(jnp.float32))
    result, pull_back = jax.vjp(forward, *primals)
    grads = pull_back(cotangent.astype(jnp.float32))
    return (result.astype(jnp.bfloat16), grads[0], grads[1], grads[2], grads[3], grads[4], grads[5], grads[6])
```

```python
import jax
import jax.numpy as jnp
from jax import lax
from jax.sharding import PartitionSpec as P

HEADS = 12
EPSILON = 1e-05
ROPE_THETA = 160000.0
NEGATIVE = -1e30
F32 = jnp.float32
BF = jnp.bfloat16


def dot(a, b):
    return jnp.dot(a, b, preferred_element_type=F32)


def dot_t(a, b):
    return lax.dot_general(a, b, (((1,), (1,)), ((), ())), preferred_element_type=F32)


def t_dot(a, b):
    return lax.dot_general(a, b, (((0,), (0,)), ((), ())), preferred_element_type=F32)


def normalise(values):
    average = jnp.mean(values, axis=-1, keepdims=True)
    centred = values - average
    spread = jnp.mean(centred * centred, axis=-1, keepdims=True)
    inverse = lax.rsqrt(spread + EPSILON)
    return centred * inverse, inverse


def normalise_back(unit, inverse, grad):
    mean_grad = jnp.mean(grad, axis=-1, keepdims=True)
    mean_both = jnp.mean(grad * unit, axis=-1, keepdims=True)
    return inverse * (grad - mean_grad - unit * mean_both)


def rope_tables(row_count, head_size, heads):
    position = jnp.arange(row_count, dtype=jnp.int32).astype(F32)
    frequency = ROPE_THETA ** (-jnp.arange(0, head_size, 2, dtype=F32) / head_size)
    angles = position[:, None] * frequency[None, :]
    angles = jnp.concatenate([angles, angles], axis=-1)
    return jnp.cos(angles), jnp.sin(angles)


def rotary(values, cosines, sines):
    half = values.shape[-1] // 2
    turned = jnp.concatenate([-values[..., half:], values[..., :half]], axis=-1)
    return values * cosines + turned * sines


def rotary_back(grads, cosines, sines):
    half = grads.shape[-1] // 2
    shifted = grads * sines
    return grads * cosines + jnp.concatenate([shifted[..., half:], -shifted[..., :half]], axis=-1)


def geglu(gate_in, gate_up):
    return jax.nn.gelu(gate_in, approximate=False) * gate_up


def gather_ctx(block, n_ctx):
    return lax.all_gather(block, "ctx", axis=0, tiled=False)


def scatter_ctx(blocks, n_ctx):
    return lax.psum_scatter(blocks, "ctx", scatter_dimension=0, tiled=False)


def gather_dp(block):
    return lax.all_gather(block, "dp", axis=0, tiled=True)


def scatter_dp(blocks):
    return lax.psum_scatter(blocks, "dp", scatter_dimension=0, tiled=True)


def round_up(n, m):
    return -(-n // m) * m


def make_local(n_dp, n_ctx):
    def local(hidden_in, segment_ids, w_qkv, w_out, w_in, w_down, gain_attn, gain_mlp, cotangent):
        rows, width = hidden_in.shape[1], hidden_in.shape[2]
        head_size = width // HEADS
        scale = head_size ** (-0.5)
        per = -(-HEADS // n_ctx)
        owners = HEADS // per
        tokens = rows * n_ctx
        shard = w_qkv.shape[0]
        hidden_units = w_in.shape[1] // 2
        down_rows = w_down.shape[0]
        own = down_rows // n_ctx
        padded = round_up(own, 16)
        units = n_dp * padded
        cols = per * head_size
        me = lax.axis_index("ctx")
        valid = me < owners
        slot = jnp.minimum(me, owners - 1)

        qkv_mine = lax.dynamic_slice(
            w_qkv.reshape(shard, 3, width), (0, 0, slot * cols), (shard, 3, cols)
        ).reshape(shard, 3 * cols)
        gains = jnp.stack([gain_attn, gain_mlp], axis=1)
        first = gather_dp(jnp.concatenate([qkv_mine, gains], axis=1))
        qkv_full = first[:, : 3 * cols]
        attn_gain = first[:, 3 * cols].astype(F32)[None, :]
        mlp_gain = first[:, 3 * cols + 1].astype(F32)[None, :]
        in_mine = lax.dynamic_slice(
            w_in.reshape(shard, 2 * n_dp, down_rows), (0, 0, me * own), (shard, 2 * n_dp, own)
        )
        in_mine = jnp.pad(in_mine, ((0, 0), (0, 0), (0, padded - own))).reshape(shard, 2 * units)
        in_full = gather_dp(in_mine)
        down_mine = lax.dynamic_slice(w_down, (me * own, 0), (own, width))
        down_full = gather_dp(jnp.pad(down_mine, ((0, padded - own), (0, 0))))
        out_full = lax.dynamic_slice(gather_dp(w_out), (slot * cols, 0), (cols, width))

        id_row = jnp.pad(segment_ids.astype(BF), ((0, 15), (0, width - rows)))
        packed = gather_ctx(jnp.concatenate([hidden_in[0], cotangent[0], id_row], axis=0), n_ctx)
        source = packed[:, :rows].reshape(tokens, width).astype(F32)
        upstream = packed[:, rows : 2 * rows].reshape(tokens, width)
        ids = packed[:, 2 * rows, :rows].reshape(tokens).astype(jnp.int32)

        cosines, sines = rope_tables(tokens, head_size, per)
        unit_one, inverse_one = normalise(source)
        normed_one = (unit_one * attn_gain).astype(BF)
        projected = dot(normed_one, qkv_full)

        def head_of(part, h):
            start = part * cols + h * head_size
            return projected[:, start : start + head_size]

        queries = jnp.stack([rotary(head_of(0, h), cosines, sines) for h in range(per)]).astype(BF)
        keys = jnp.stack([rotary(head_of(1, h), cosines, sines) for h in range(per)]).astype(BF)
        values = jnp.stack([head_of(2, h) for h in range(per)]).astype(BF)
        chunk = min(tokens, 1024)
        pieces = tokens // chunk
        attention, log_total = [], []
        for c in range(pieces):
            part = slice(c * chunk, (c + 1) * chunk)
            scores = jnp.einsum("hqe,hke->hqk", queries[:, part], keys, preferred_element_type=F32) * scale
            allowed = (ids[part][:, None] == ids[None, :])[None]
            scores = jnp.where(allowed, scores, NEGATIVE)
            highest = jnp.max(scores, axis=-1, keepdims=True)
            weights = jnp.where(allowed, jnp.exp(scores - highest), 0.0)
            total = jnp.sum(weights, axis=-1, keepdims=True)
            summed = jnp.einsum("hqk,hke->hqe", weights.astype(BF), values, preferred_element_type=F32)
            attention.append(summed / total)
            log_total.append(highest + jnp.log(total))
        attention_all = jnp.concatenate(attention, axis=1)
        attention_all = jnp.where(valid, attention_all, 0.0)
        attended = jnp.concatenate([attention_all[h] for h in range(per)], axis=1).astype(BF)
        branch = scatter_ctx(dot(attended, out_full).astype(BF).reshape(n_ctx, rows, width), n_ctx)
        middle = hidden_in[0].astype(F32) + branch.astype(F32)
        unit_two, inverse_two = normalise(middle)
        normed_two = gather_ctx((unit_two * mlp_gain).astype(BF), n_ctx).reshape(tokens, width)
        lifted = dot(normed_two, in_full)
        gate_in, gate_up = lifted[:, :units], lifted[:, units:]
        mixed_value, pull_gate = jax.vjp(geglu, gate_in, gate_up)
        mixed_units = mixed_value.astype(BF)
        out_part = dot(mixed_units, down_full).astype(BF)
        grad_gate_in, grad_gate_up = pull_gate(dot_t(upstream, down_full))
        grad_lifted = jnp.concatenate([grad_gate_in, grad_gate_up], axis=1).astype(BF)
        grad_normed_part = dot_t(grad_lifted, in_full).astype(BF)
        both = jnp.concatenate(
            [out_part.reshape(n_ctx, rows, width), grad_normed_part.reshape(n_ctx, rows, width)], axis=1
        )
        both = scatter_ctx(both, n_ctx).astype(F32)
        grad_in = scatter_dp(t_dot(normed_two, grad_lifted).astype(BF))
        grad_down = scatter_dp(t_dot(mixed_units, upstream).astype(BF))
        result = (middle + both[:rows]).astype(BF)
        grad_normed_two = both[rows:]
        gain_part = jnp.sum(grad_normed_two * unit_two, axis=0, keepdims=True)
        grad_middle = cotangent[0].astype(F32) + normalise_back(
            unit_two, inverse_two, grad_normed_two * mlp_gain
        )
        gain_rows = jnp.pad(gain_part.astype(BF), ((0, 15), (0, 0)))
        sent = gather_ctx(jnp.concatenate([grad_middle.astype(BF), gain_rows], axis=0), n_ctx)
        grad_branch = sent[:, :rows].reshape(tokens, width)
        mlp_gain_sum = jnp.sum(sent[:, rows].astype(F32), axis=0)
        grad_attended = dot_t(grad_branch, out_full)
        grad_heads = jnp.stack(
            [grad_attended[:, h * head_size : (h + 1) * head_size] for h in range(per)]
        ).astype(BF)
        grad_out = t_dot(attended, grad_branch).astype(BF)
        grad_queries, grad_keys, grad_values = [], 0.0, 0.0
        for c in range(pieces):
            part = slice(c * chunk, (c + 1) * chunk)
            scores = jnp.einsum("hqe,hke->hqk", queries[:, part], keys, preferred_element_type=F32) * scale
            allowed = (ids[part][:, None] == ids[None, :])[None]
            probs = jnp.where(allowed, jnp.exp(scores - log_total[c]), 0.0)
            grad_part = grad_heads[:, part]
            products = jnp.sum(grad_part.astype(F32) * attention_all[:, part], axis=-1, keepdims=True)
            grad_probs = jnp.einsum("hqe,hke->hqk", grad_part, values, preferred_element_type=F32)
            grad_scores = (probs * (grad_probs - products)).astype(BF)
            grad_queries.append(
                scale * jnp.einsum("hqk,hke->hqe", grad_scores, keys, preferred_element_type=F32)
            )
            grad_keys += scale * jnp.einsum(
                "hqk,hqe->hke", grad_scores, queries[:, part], preferred_element_type=F32
            )
            grad_values += jnp.einsum(
                "hqk,hqe->hke", probs.astype(BF), grad_part, preferred_element_type=F32
            )
        grad_queries = jnp.concatenate(grad_queries, axis=1)
        grad_projected = jnp.concatenate(
            [rotary_back(grad_queries[h], cosines, sines) for h in range(per)]
            + [rotary_back(grad_keys[h], cosines, sines) for h in range(per)]
            + [grad_values[h] for h in range(per)],
            axis=1,
        )
        grad_projected = jnp.where(valid, grad_projected, 0.0).astype(BF)
        grad_normed_one = dot_t(grad_projected, qkv_full)
        attn_gain_part = jnp.sum(grad_normed_one * unit_one, axis=0)
        back = scatter_ctx(grad_normed_one.astype(BF).reshape(n_ctx, rows, width), n_ctx).astype(F32)
        grad_qkv = t_dot(normed_one, grad_projected)
        last = scatter_dp(
            jnp.concatenate([grad_qkv, attn_gain_part[:, None]], axis=1).astype(BF)
        )
        out_all = gather_ctx(grad_out, n_ctx)[:owners].reshape(width, width)
        out_share = scatter_dp(
            jnp.concatenate([out_all, mlp_gain_sum[:, None].astype(BF)], axis=1)
        )
        unit_own, inverse_own = normalise(hidden_in[0].astype(F32))
        grad_input = grad_middle + normalise_back(unit_own, inverse_own, back * attn_gain)

        last_all = gather_ctx(last, n_ctx)
        share_qkv = last_all[:owners, :, : 3 * cols].reshape(owners, shard, 3, cols)
        share_qkv = jnp.transpose(share_qkv, (1, 2, 0, 3)).reshape(shard, 3 * width).astype(F32)
        share_attn = jnp.sum(last_all[:, :, 3 * cols].astype(F32), axis=0)
        share_out = out_share[:, :width].astype(F32)
        share_mlp = out_share[:, width].astype(F32)
        in_all = gather_ctx(grad_in, n_ctx).reshape(n_ctx, shard, 2 * n_dp, padded)[..., :own]
        share_in = jnp.transpose(in_all, (1, 2, 0, 3)).reshape(shard, 2 * hidden_units).astype(F32)
        down_all = gather_ctx(grad_down, n_ctx)[:, :own]
        share_down = down_all.reshape(down_rows, width).astype(F32)
        return (
            result[None],
            grad_input[None],
            share_qkv,
            share_out,
            share_in,
            share_down,
            share_attn,
            share_mlp,
        )

    return local


def solution(mesh):
    tokens = P("dp", "ctx", None)
    weight = P("dp", None)
    in_specs = (tokens, P("dp", "ctx")) + (weight,) * 4 + (P("dp"), P("dp"), tokens)
    out_specs = (tokens, tokens) + (weight,) * 4 + (P("dp"), P("dp"))
    return jax.shard_map(
        make_local(mesh.shape["dp"], mesh.shape["ctx"]),
        mesh=mesh,
        in_specs=in_specs,
        out_specs=out_specs,
        check_vma=False,
    )
```

```python
import math

import jax
import jax.numpy as jnp
from jax import lax
from jax.experimental import pallas as pl
from jax.experimental.pallas import tpu as pltpu
from jax.sharding import PartitionSpec as P

HEADS = 12
EPSILON = 1e-05
ROPE_THETA = 160000.0
NEGATIVE = -1e30
F32 = jnp.float32
BF = jnp.bfloat16


def dot(a, b):
    return jnp.dot(a, b, preferred_element_type=F32)


def dot_t(a, b):
    return lax.dot_general(a, b, (((1,), (1,)), ((), ())), preferred_element_type=F32)


def t_dot(a, b):
    return lax.dot_general(a, b, (((0,), (0,)), ((), ())), preferred_element_type=F32)


def normalise(values):
    average = jnp.mean(values, axis=-1, keepdims=True)
    centred = values - average
    spread = jnp.mean(centred * centred, axis=-1, keepdims=True)
    inverse = lax.rsqrt(spread + EPSILON)
    return centred * inverse, inverse


def normalise_back(unit, inverse, grad):
    mean_grad = jnp.mean(grad, axis=-1, keepdims=True)
    mean_both = jnp.mean(grad * unit, axis=-1, keepdims=True)
    return inverse * (grad - mean_grad - unit * mean_both)


def rope_tables(row_count, head_size, heads):
    position = jnp.arange(row_count, dtype=jnp.int32).astype(F32)
    frequency = ROPE_THETA ** (-jnp.arange(0, head_size, 2, dtype=F32) / head_size)
    angles = position[:, None] * frequency[None, :]
    angles = jnp.concatenate([angles, angles], axis=-1)
    return jnp.cos(angles), jnp.sin(angles)


def rotary(values, cosines, sines):
    half = values.shape[-1] // 2
    turned = jnp.concatenate([-values[..., half:], values[..., :half]], axis=-1)
    return values * cosines + turned * sines


def rotary_back(grads, cosines, sines):
    half = grads.shape[-1] // 2
    shifted = grads * sines
    return grads * cosines + jnp.concatenate([shifted[..., half:], -shifted[..., :half]], axis=-1)


def geglu(gate_in, gate_up):
    return jax.nn.gelu(gate_in, approximate=False) * gate_up


MESH = pl.DeviceIdType.MESH


class Places:
    def __init__(self, n_dp, n_ctx, send_sem, recv_sem):
        self.n_dp, self.n_ctx, self.chips = n_dp, n_ctx, n_ctx // 2
        self.z = lax.axis_index("dp")
        self.me = lax.axis_index("ctx")
        self.chip, self.core = self.me // 2, self.me % 2
        self.sibling = self.chip * 2 + 1 - self.core
        self.send_sem, self.recv_sem, self.used = send_sem, recv_sem, 0

    def other_chip(self, d):
        return jnp.bitwise_xor(self.chip, d)

    def other_dp(self, d):
        return jnp.bitwise_xor(self.z, d)

    def copy(self, src, dst, z, ctx):
        k = self.used
        self.used += 1
        return pltpu.make_async_remote_copy(
            src_ref=src,
            dst_ref=dst,
            send_sem=self.send_sem.at[k],
            recv_sem=self.recv_sem.at[k],
            device_id=(z, ctx),
            device_id_type=MESH,
        )


def run_gather_ctx(p, src, out):
    first, second = [], []
    for d in range(1, p.chips):
        peer = p.other_chip(d) * 2 + p.core
        first.append(p.copy(src, out.at[p.me], p.z, peer))
        first[-1].start()
    near = p.copy(src, out.at[p.me], p.z, p.sibling)
    near.start()
    out[p.me] = src[...]
    yield
    for d in range(1, p.chips):
        first[d - 1].wait_recv()
        held = out.at[p.other_chip(d) * 2 + p.core]
        second.append(p.copy(held, held, p.z, p.sibling))
        second[-1].start()
        yield
    for item in first:
        item.wait_send()
    near.wait()
    for item in second:
        item.wait()


def run_scatter_ctx(p, src, out, sib, acc, land):
    near, far = [], []
    for d in list(range(1, p.chips)) + [0]:
        chip = p.other_chip(d)
        near.append(p.copy(src.at[chip * 2 + 1 - p.core], sib.at[d], p.z, p.sibling))
        near[-1].start()
    yield
    for d in range(1, p.chips):
        near[d - 1].wait_recv()
        chip = p.other_chip(d)
        acc[d] = (src[chip * 2 + p.core].astype(F32) + sib[d].astype(F32)).astype(acc.dtype)
        far.append(p.copy(acc.at[d], land.at[d], p.z, chip * 2 + p.core))
        far[-1].start()
    near[-1].wait_recv()
    out[...] = src[p.me].astype(F32) + sib[0].astype(F32)
    yield
    for d in range(1, p.chips):
        far[d - 1].wait_recv()
        out[...] += land[d].astype(F32)
    for item in far + near:
        item.wait_send()


def run_gather_dp(p, src, out):
    copies = []
    for d in range(1, p.n_dp):
        copies.append(p.copy(src, out.at[p.z], p.other_dp(d), p.me))
        copies[-1].start()
    out[p.z] = src[...]
    yield
    for item in copies:
        item.wait()


def run_scatter_dp(p, src, out, land):
    copies = []
    for d in range(1, p.n_dp):
        copies.append(p.copy(src.at[p.other_dp(d)], land.at[d], p.other_dp(d), p.me))
        copies[-1].start()
    yield
    total = src[p.z].astype(F32)
    for d in range(1, p.n_dp):
        copies[d - 1].wait_recv()
        total = total + land[d].astype(F32)
    out[...] = total.astype(out.dtype)
    for item in copies:
        item.wait_send()


def run_reduce(p, src, out, land, mid):
    yield from run_scatter_dp(p, src, mid, land)
    yield from run_gather_ctx(p, mid, out)


def head_place(p, s, per):
    owners = HEADS // per
    head = jnp.minimum(p.me, owners - 1) * per + s
    each = HEADS // p.n_dp
    return head // each, head % each


def run_rows_gather(p, src, out, per):
    size = out.shape[0] // per
    jobs = []
    for s in range(per):
        owner, place = head_place(p, s, per)
        rows = src.at[pl.ds(pl.multiple_of(place * size, size), size)]
        slot = out.at[pl.ds(s * size, size)]
        copies = [p.copy(rows, slot, p.other_dp(d), p.me) for d in range(1, p.n_dp)]
        jobs.append((owner, copies))

        @pl.when(p.z == owner)
        def _():
            for item in copies:
                item.start()
            out[pl.ds(s * size, size)] = src[pl.ds(pl.multiple_of(place * size, size), size)]

    yield
    for owner, copies in jobs:
        for d in range(1, p.n_dp):
            item = copies[d - 1]

            @pl.when(p.z == owner)
            def _():
                item.wait_send()

            @pl.when(p.other_dp(d) == owner)
            def _():
                item.wait_recv()


def run_rows_scatter(p, src, out, land, per):
    size = src.shape[0] // per
    jobs = []
    for s in range(per):
        owner, _ = head_place(p, s, per)
        slot = pl.ds(s * size, size)
        copies = [
            p.copy(src.at[slot], land.at[d, slot], p.other_dp(d), p.me) for d in range(1, p.n_dp)
        ]
        jobs.append((owner, slot, copies))
        for d in range(1, p.n_dp):
            item = copies[d - 1]

            @pl.when(p.other_dp(d) == owner)
            def _():
                item.start()

    yield
    for owner, slot, copies in jobs:

        @pl.when(p.z == owner)
        def _():
            total = src[slot].astype(F32)
            for d in range(1, p.n_dp):
                copies[d - 1].wait_recv()
                total = total + land[d, slot].astype(F32)
            out[slot] = total.astype(out.dtype)

        @pl.when(p.z != owner)
        def _():
            out[slot] = src[slot]

        for d in range(1, p.n_dp):
            item = copies[d - 1]

            @pl.when(p.other_dp(d) == owner)
            def _():
                item.wait_send()


def exchange(tasks, n_dp, n_ctx, collective):
    chips = n_ctx // 2
    per = -(-HEADS // n_ctx)
    outs, scratch, counts, runs, copies = [], [], [], [], 0
    for kind, array in tasks:
        shape, more, kept = array.shape, [], array.dtype
        if kind == "gather_ctx":
            shape, run, n = (n_ctx,) + shape, run_gather_ctx, 2 * chips - 1
        elif kind == "scatter_ctx":
            shape, run, n, kept = shape[1:], run_scatter_ctx, 2 * chips - 1, F32
            more = [(chips,) + shape] * 3
        elif kind == "gather_dp":
            shape, run, n = (n_dp,) + shape, run_gather_dp, n_dp - 1
        elif kind == "scatter_dp":
            shape, run, n = shape[1:], run_scatter_dp, n_dp - 1
            more = [(n_dp,) + shape]
        elif kind == "reduce":
            more = [shape, shape[1:]]
            shape, run, n = (n_ctx,) + shape[1:], run_reduce, n_dp - 1 + 2 * chips - 1
        elif kind == "rows_gather":
            width = shape[1]
            shape, n = (per * (width // HEADS), width), per * (n_dp - 1)
            run = lambda *a: run_rows_gather(*a, per)
        elif kind == "rows_scatter":
            more, n = [(n_dp,) + shape], per * (n_dp - 1)
            run = lambda *a: run_rows_scatter(*a, per)
        outs.append(jax.ShapeDtypeStruct(shape, kept))
        scratch += [pltpu.VMEM(m, array.dtype) for m in more]
        counts.append(len(more))
        runs.append(run)
        copies += n
    kinds = [kind for kind, _ in tasks]
    use_ctx = any(k in ("gather_ctx", "scatter_ctx", "reduce") for k in kinds)
    use_dp = any(k not in ("gather_ctx", "scatter_ctx") for k in kinds)

    def kernel(*refs):
        n = len(tasks)
        ins, results, rest = refs[:n], refs[n : 2 * n], list(refs[2 * n :])
        send_sem, recv_sem = rest[-2:]
        p = Places(n_dp, n_ctx, send_sem, recv_sem)
        barrier = pltpu.get_barrier_semaphore()
        partners = []
        if use_ctx:
            partners.append((p.z, p.sibling))
            partners += [(p.z, p.other_chip(d) * 2 + p.core) for d in range(1, chips)]
        if use_dp:
            partners += [(p.other_dp(d), p.me) for d in range(1, n_dp)]
        for partner in partners:
            pl.semaphore_signal(barrier, inc=1, device_id=partner, device_id_type=MESH)
        pl.semaphore_wait(barrier, len(partners))
        live = []
        for i in range(n):
            mine, rest = rest[: counts[i]], rest[counts[i] :]
            live.append(runs[i](p, ins[i], results[i], *mine))
        while live:
            for task in list(live):
                try:
                    next(task)
                except StopIteration:
                    live.remove(task)

    size = lambda shape: 2 * (math.prod(shape[:-1]) + 16) * round_up(shape[-1], 128)
    need = sum(size(a.shape) for _, a in tasks) + sum(2 * size(o.shape) for o in outs)
    need += sum(size(m.shape) for m in scratch)
    sent = sum(size(a.shape) for _, a in tasks)
    vmem = pl.BlockSpec(memory_space=pltpu.VMEM)
    return pl.pallas_call(
        kernel,
        out_shape=outs,
        in_specs=[vmem] * len(tasks),
        out_specs=[vmem] * len(tasks),
        scratch_shapes=scratch
        + [pltpu.SemaphoreType.DMA((copies,)), pltpu.SemaphoreType.DMA((copies,))],
        compiler_params=pltpu.CompilerParams(
            collective_id=collective,
            has_side_effects=True,
            vmem_limit_bytes=min(60 << 20, max(16 << 20, need + need // 4 + (4 << 20))),
        ),
        cost_estimate=pl.CostEstimate(flops=0, bytes_accessed=4 * sent, transcendentals=0),
    )(*[a for _, a in tasks])


def round_up(n, m):
    return -(-n // m) * m


def make_local(n_dp, n_ctx):
    def local(hidden_in, segment_ids, w_qkv, w_out, w_in, w_down, gain_attn, gain_mlp, cotangent):
        rows, width = hidden_in.shape[1], hidden_in.shape[2]
        head_size = width // HEADS
        scale = head_size ** (-0.5)
        per = -(-HEADS // n_ctx)
        owners = HEADS // per
        tokens = rows * n_ctx
        shard = w_qkv.shape[0]
        hidden_units = w_in.shape[1] // 2
        down_rows = w_down.shape[0]
        own = down_rows // n_ctx
        padded = round_up(own, 16)
        units = n_dp * padded
        cols = per * head_size
        me = lax.axis_index("ctx")
        valid = me < owners
        slot = jnp.minimum(me, owners - 1)

        qkv_mine = lax.dynamic_slice(
            w_qkv.reshape(shard, 3, width), (0, 0, slot * cols), (shard, 3, cols)
        ).reshape(shard, 3 * cols)
        gains = jnp.pad(jnp.stack([gain_attn, gain_mlp]), ((0, 14), (0, 0)))
        in_mine = lax.dynamic_slice(
            w_in.reshape(shard, 2 * n_dp, down_rows), (0, 0, me * own), (shard, 2 * n_dp, own)
        )
        in_mine = jnp.pad(in_mine, ((0, 0), (0, 0), (0, padded - own))).reshape(shard, 2 * units)
        down_mine = jnp.pad(
            lax.dynamic_slice(w_down, (me * own, 0), (own, width)), ((0, padded - own), (0, 0))
        )
        id_row = jnp.pad(segment_ids.astype(BF), ((0, 15), (0, 0)))
        hidden_all, qkv_full, gains_all, id_all, out_full, upstream = exchange(
            [
                ("gather_ctx", hidden_in[0]),
                ("gather_dp", qkv_mine),
                ("gather_dp", gains),
                ("gather_ctx", id_row),
                ("rows_gather", w_out),
                ("gather_ctx", cotangent[0]),
            ],
            n_dp, n_ctx, 0,
        )
        qkv_full = qkv_full.reshape(width, 3 * cols)
        attn_gain = gains_all[:, 0].reshape(1, width).astype(F32)
        mlp_gain = gains_all[:, 1].reshape(1, width).astype(F32)
        source = hidden_all.reshape(tokens, width).astype(F32)
        upstream = upstream.reshape(tokens, width)
        ids = id_all[:, 0].reshape(tokens).astype(jnp.int32)

        cosines, sines = rope_tables(tokens, head_size, per)
        unit_one, inverse_one = normalise(source)
        normed_one = (unit_one * attn_gain).astype(BF)
        projected = dot(normed_one, qkv_full)

        def head_of(part, h):
            start = part * cols + h * head_size
            return projected[:, start : start + head_size]

        queries = jnp.stack([rotary(head_of(0, h), cosines, sines) for h in range(per)]).astype(BF)
        keys = jnp.stack([rotary(head_of(1, h), cosines, sines) for h in range(per)]).astype(BF)
        values = jnp.stack([head_of(2, h) for h in range(per)]).astype(BF)
        chunk = min(tokens, 1024)
        pieces = tokens // chunk
        attention, log_total = [], []
        for c in range(pieces):
            part = slice(c * chunk, (c + 1) * chunk)
            scores = jnp.einsum("hqe,hke->hqk", queries[:, part], keys, preferred_element_type=F32) * scale
            allowed = (ids[part][:, None] == ids[None, :])[None]
            scores = jnp.where(allowed, scores, NEGATIVE)
            highest = jnp.max(scores, axis=-1, keepdims=True)
            weights = jnp.where(allowed, jnp.exp(scores - highest), 0.0)
            total = jnp.sum(weights, axis=-1, keepdims=True)
            summed = jnp.einsum("hqk,hke->hqe", weights.astype(BF), values, preferred_element_type=F32)
            attention.append(summed / total)
            log_total.append(highest + jnp.log(total))
        attention_all = jnp.concatenate(attention, axis=1)
        attention_all = jnp.where(valid, attention_all, 0.0)
        attended = jnp.concatenate([attention_all[h] for h in range(per)], axis=1).astype(BF)
        branch, in_full = exchange(
            [
                ("scatter_ctx", dot(attended, out_full).astype(BF).reshape(n_ctx, rows, width)),
                ("gather_dp", in_mine),
            ],
            n_dp, n_ctx, 1,
        )
        in_full = in_full.reshape(width, 2 * units)
        middle = hidden_in[0].astype(F32) + branch
        unit_two, inverse_two = normalise(middle)
        normed_two, down_full = exchange(
            [("gather_ctx", (unit_two * mlp_gain).astype(BF)), ("gather_dp", down_mine)],
            n_dp, n_ctx, 2,
        )
        normed_two = normed_two.reshape(tokens, width)
        down_full = down_full.reshape(units, width)
        lifted = dot(normed_two, in_full)
        gate_in, gate_up = lifted[:, :units], lifted[:, units:]
        mixed_value, pull_gate = jax.vjp(geglu, gate_in, gate_up)
        mixed_units = mixed_value.astype(BF)
        out_part = dot(mixed_units, down_full).astype(BF)
        grad_gate_in, grad_gate_up = pull_gate(dot_t(upstream, down_full))
        grad_lifted = jnp.concatenate([grad_gate_in, grad_gate_up], axis=1).astype(BF)
        grad_normed_part = dot_t(grad_lifted, in_full).astype(BF)
        out_sum, grad_normed_two = exchange(
            [
                ("scatter_ctx", grad_normed_part.reshape(n_ctx, rows, width)),
                ("scatter_ctx", out_part.reshape(n_ctx, rows, width)),
            ][::-1],
            n_dp, n_ctx, 3,
        )
        grad_in = t_dot(normed_two, grad_lifted).astype(BF).reshape(n_dp, shard, 2 * units)
        grad_down = t_dot(mixed_units, upstream).astype(BF).reshape(n_dp, padded, width)
        result = (middle + out_sum).astype(BF)
        gain_part = jnp.sum(grad_normed_two * unit_two, axis=0, keepdims=True)
        grad_middle = cotangent[0].astype(F32) + normalise_back(
            unit_two, inverse_two, grad_normed_two * mlp_gain
        )
        gain_rows = jnp.pad(gain_part.astype(BF), ((0, 15), (0, 0)))
        grad_branch, gain_rows, grad_in = exchange(
            [
                ("gather_ctx", grad_middle.astype(BF)),
                ("gather_ctx", gain_rows),
                ("scatter_dp", grad_in),
            ],
            n_dp, n_ctx, 4,
        )
        grad_branch = grad_branch.reshape(tokens, width)
        mlp_gain_sum = jnp.sum(gain_rows[:, 0].astype(F32), axis=0)
        grad_attended = dot_t(grad_branch, out_full)
        grad_heads = jnp.stack(
            [grad_attended[:, h * head_size : (h + 1) * head_size] for h in range(per)]
        ).astype(BF)
        grad_out = t_dot(attended, grad_branch).astype(BF)
        grad_queries, grad_keys, grad_values = [], 0.0, 0.0
        for c in range(pieces):
            part = slice(c * chunk, (c + 1) * chunk)
            scores = jnp.einsum("hqe,hke->hqk", queries[:, part], keys, preferred_element_type=F32) * scale
            allowed = (ids[part][:, None] == ids[None, :])[None]
            probs = jnp.where(allowed, jnp.exp(scores - log_total[c]), 0.0)
            grad_part = grad_heads[:, part]
            products = jnp.sum(grad_part.astype(F32) * attention_all[:, part], axis=-1, keepdims=True)
            grad_probs = jnp.einsum("hqe,hke->hqk", grad_part, values, preferred_element_type=F32)
            grad_scores = (probs * (grad_probs - products)).astype(BF)
            grad_queries.append(
                scale * jnp.einsum("hqk,hke->hqe", grad_scores, keys, preferred_element_type=F32)
            )
            grad_keys += scale * jnp.einsum(
                "hqk,hqe->hke", grad_scores, queries[:, part], preferred_element_type=F32
            )
            grad_values += jnp.einsum(
                "hqk,hqe->hke", probs.astype(BF), grad_part, preferred_element_type=F32
            )
        grad_queries = jnp.concatenate(grad_queries, axis=1)
        grad_projected = jnp.concatenate(
            [rotary_back(grad_queries[h], cosines, sines) for h in range(per)]
            + [rotary_back(grad_keys[h], cosines, sines) for h in range(per)]
            + [grad_values[h] for h in range(per)],
            axis=1,
        )
        grad_projected = jnp.where(valid, grad_projected, 0.0).astype(BF)
        grad_normed_one = dot_t(grad_projected, qkv_full)
        attn_gain_part = jnp.sum(grad_normed_one * unit_one, axis=0)
        back, grad_down, grad_out, in_all = exchange(
            [
                ("scatter_ctx", grad_normed_one.astype(BF).reshape(n_ctx, rows, width)),
                ("scatter_dp", grad_down),
                ("rows_scatter", grad_out),
                ("gather_ctx", grad_in),
            ],
            n_dp, n_ctx, 5,
        )
        grad_qkv = t_dot(normed_one, grad_projected).astype(BF).reshape(n_dp, shard, 3 * cols)
        gain_sums = jnp.stack([attn_gain_part, mlp_gain_sum]).astype(BF).reshape(2, n_dp, shard)
        gain_sums = jnp.pad(jnp.transpose(gain_sums, (1, 0, 2)), ((0, 0), (0, 14), (0, 0)))
        last_all, gains_last, out_all, down_all = exchange(
            [
                ("reduce", grad_qkv),
                ("reduce", gain_sums),
                ("gather_ctx", grad_out),
                ("gather_ctx", grad_down),
            ],
            n_dp, n_ctx, 6,
        )
        unit_own, inverse_own = normalise(hidden_in[0].astype(F32))
        grad_input = grad_middle + normalise_back(unit_own, inverse_own, back * attn_gain)

        share_qkv = last_all[:owners].reshape(owners, shard, 3, cols)
        share_qkv = jnp.transpose(share_qkv, (1, 2, 0, 3)).reshape(shard, 3 * width).astype(F32)
        share_attn = jnp.sum(gains_last[:, 0].astype(F32), axis=0)
        share_mlp = gains_last[0, 1].astype(F32)
        out_rows = width // n_dp
        share_out = lax.dynamic_slice(
            out_all.reshape(n_ctx * cols, width), (lax.axis_index("dp") * out_rows, 0), (out_rows, width)
        ).astype(F32)
        in_all = in_all.reshape(n_ctx, shard, 2 * n_dp, padded)[..., :own]
        share_in = jnp.transpose(in_all, (1, 2, 0, 3)).reshape(shard, 2 * hidden_units).astype(F32)
        share_down = down_all[:, :own].reshape(down_rows, width).astype(F32)
        return (
            result[None],
            grad_input[None],
            share_qkv,
            share_out,
            share_in,
            share_down,
            share_attn,
            share_mlp,
        )

    return local


def solution(mesh):
    tokens = P("dp", "ctx", None)
    weight = P("dp", None)
    in_specs = (tokens, P("dp", "ctx")) + (weight,) * 4 + (P("dp"), P("dp"), tokens)
    out_specs = (tokens, tokens) + (weight,) * 4 + (P("dp"), P("dp"))
    return jax.shard_map(
        make_local(mesh.shape["dp"], mesh.shape["ctx"]),
        mesh=mesh,
        in_specs=in_specs,
        out_specs=out_specs,
        check_vma=False,
    )
```

```python
import math

import jax
import jax.numpy as jnp
from jax import lax
from jax.experimental import pallas as pl
from jax.experimental.pallas import tpu as pltpu
from jax.sharding import PartitionSpec as P

HEADS = 12
EPSILON = 1e-05
ROPE_THETA = 160000.0
NEGATIVE = -1e30
F32 = jnp.float32
BF = jnp.bfloat16


def dot(a, b):
    return jnp.dot(a, b, preferred_element_type=F32)


def dot_t(a, b):
    return lax.dot_general(a, b, (((1,), (1,)), ((), ())), preferred_element_type=F32)


def t_dot(a, b):
    return lax.dot_general(a, b, (((0,), (0,)), ((), ())), preferred_element_type=F32)


def normalise(values):
    average = jnp.mean(values, axis=-1, keepdims=True)
    centred = values - average
    spread = jnp.mean(centred * centred, axis=-1, keepdims=True)
    inverse = lax.rsqrt(spread + EPSILON)
    return centred * inverse, inverse


def normalise_back(unit, inverse, grad):
    mean_grad = jnp.mean(grad, axis=-1, keepdims=True)
    mean_both = jnp.mean(grad * unit, axis=-1, keepdims=True)
    return inverse * (grad - mean_grad - unit * mean_both)


def rope_tables(row_count, head_size, heads):
    position = jnp.arange(row_count, dtype=jnp.int32).astype(F32)
    frequency = ROPE_THETA ** (-jnp.arange(0, head_size, 2, dtype=F32) / head_size)
    angles = position[:, None] * frequency[None, :]
    angles = jnp.concatenate([angles, angles], axis=-1)
    return jnp.cos(angles), jnp.sin(angles)


def rotary(values, cosines, sines):
    half = values.shape[-1] // 2
    turned = jnp.concatenate([-values[..., half:], values[..., :half]], axis=-1)
    return values * cosines + turned * sines


def rotary_back(grads, cosines, sines):
    half = grads.shape[-1] // 2
    shifted = grads * sines
    return grads * cosines + jnp.concatenate([shifted[..., half:], -shifted[..., :half]], axis=-1)


def geglu(gate_in, gate_up):
    return jax.nn.gelu(gate_in, approximate=False) * gate_up


MESH = pl.DeviceIdType.MESH


class Places:
    def __init__(self, n_dp, n_ctx, send_sem, recv_sem):
        self.n_dp, self.n_ctx, self.chips = n_dp, n_ctx, n_ctx // 2
        self.z = lax.axis_index("dp")
        self.me = lax.axis_index("ctx")
        self.chip, self.core = self.me // 2, self.me % 2
        self.sibling = self.chip * 2 + 1 - self.core
        self.send_sem, self.recv_sem, self.used = send_sem, recv_sem, 0

    def other_chip(self, d):
        return jnp.bitwise_xor(self.chip, d)

    def other_dp(self, d):
        return jnp.bitwise_xor(self.z, d)

    def copy(self, src, dst, z, ctx):
        k = self.used
        self.used += 1
        return pltpu.make_async_remote_copy(
            src_ref=src,
            dst_ref=dst,
            send_sem=self.send_sem.at[k],
            recv_sem=self.recv_sem.at[k],
            device_id=(z, ctx),
            device_id_type=MESH,
        )


def run_gather_ctx(p, src, out):
    first, second = [], []
    for d in range(1, p.chips):
        peer = p.other_chip(d) * 2 + p.core
        first.append(p.copy(src, out.at[p.me], p.z, peer))
        first[-1].start()
    near = p.copy(src, out.at[p.me], p.z, p.sibling)
    near.start()
    out[p.me] = src[...]
    yield
    for d in range(1, p.chips):
        first[d - 1].wait_recv()
        held = out.at[p.other_chip(d) * 2 + p.core]
        second.append(p.copy(held, held, p.z, p.sibling))
        second[-1].start()
        yield
    for item in first:
        item.wait_send()
    near.wait()
    for item in second:
        item.wait()


def run_scatter_ctx(p, src, out, sib, acc, land):
    near, far = [], []
    for d in list(range(1, p.chips)) + [0]:
        chip = p.other_chip(d)
        near.append(p.copy(src.at[chip * 2 + 1 - p.core], sib.at[d], p.z, p.sibling))
        near[-1].start()
    yield
    for d in range(1, p.chips):
        near[d - 1].wait_recv()
        chip = p.other_chip(d)
        acc[d] = (src[chip * 2 + p.core].astype(F32) + sib[d].astype(F32)).astype(acc.dtype)
        far.append(p.copy(acc.at[d], land.at[d], p.z, chip * 2 + p.core))
        far[-1].start()
    near[-1].wait_recv()
    out[...] = src[p.me].astype(F32) + sib[0].astype(F32)
    yield
    for d in range(1, p.chips):
        far[d - 1].wait_recv()
        out[...] += land[d].astype(F32)
    for item in far + near:
        item.wait_send()


def run_gather_dp(p, src, out):
    copies = []
    for d in range(1, p.n_dp):
        copies.append(p.copy(src, out.at[p.z], p.other_dp(d), p.me))
        copies[-1].start()
    out[p.z] = src[...]
    yield
    for item in copies:
        item.wait()


def run_scatter_dp(p, src, out, land):
    copies = []
    for d in range(1, p.n_dp):
        copies.append(p.copy(src.at[p.other_dp(d)], land.at[d], p.other_dp(d), p.me))
        copies[-1].start()
    yield
    total = src[p.z].astype(F32)
    for d in range(1, p.n_dp):
        copies[d - 1].wait_recv()
        total = total + land[d].astype(F32)
    out[...] = total.astype(out.dtype)
    for item in copies:
        item.wait_send()


def run_reduce(p, src, out, land, mid):
    yield from run_scatter_dp(p, src, mid, land)
    yield from run_gather_ctx(p, mid, out)


def head_place(p, s, per):
    owners = HEADS // per
    head = jnp.minimum(p.me, owners - 1) * per + s
    each = HEADS // p.n_dp
    return head // each, head % each


def run_rows_gather(p, src, out, per):
    size = out.shape[0] // per
    jobs = []
    for s in range(per):
        owner, place = head_place(p, s, per)
        rows = src.at[pl.ds(pl.multiple_of(place * size, size), size)]
        slot = out.at[pl.ds(s * size, size)]
        copies = [p.copy(rows, slot, p.other_dp(d), p.me) for d in range(1, p.n_dp)]
        jobs.append((owner, copies))

        @pl.when(p.z == owner)
        def _():
            for item in copies:
                item.start()
            out[pl.ds(s * size, size)] = src[pl.ds(pl.multiple_of(place * size, size), size)]

    yield
    for owner, copies in jobs:
        for d in range(1, p.n_dp):
            item = copies[d - 1]

            @pl.when(p.z == owner)
            def _():
                item.wait_send()

            @pl.when(p.other_dp(d) == owner)
            def _():
                item.wait_recv()


def run_rows_scatter(p, src, out, land, per):
    size = src.shape[0] // per
    jobs = []
    for s in range(per):
        owner, _ = head_place(p, s, per)
        slot = pl.ds(s * size, size)
        copies = [
            p.copy(src.at[slot], land.at[d, slot], p.other_dp(d), p.me) for d in range(1, p.n_dp)
        ]
        jobs.append((owner, slot, copies))
        for d in range(1, p.n_dp):
            item = copies[d - 1]

            @pl.when(p.other_dp(d) == owner)
            def _():
                item.start()

    yield
    for owner, slot, copies in jobs:

        @pl.when(p.z == owner)
        def _():
            total = src[slot].astype(F32)
            for d in range(1, p.n_dp):
                copies[d - 1].wait_recv()
                total = total + land[d, slot].astype(F32)
            out[slot] = total.astype(out.dtype)

        @pl.when(p.z != owner)
        def _():
            out[slot] = src[slot]

        for d in range(1, p.n_dp):
            item = copies[d - 1]

            @pl.when(p.other_dp(d) == owner)
            def _():
                item.wait_send()


def place_columns(parts, own):
    def place(buf, res):
        n, width = buf.shape[0], buf.shape[2] // parts
        for j in range(n):
            block = buf[j].astype(F32)
            for p in range(parts):
                res[:, (p * n + j) * own : (p * n + j + 1) * own] = block[:, p * width : p * width + own]

    return place


def place_rows(own):
    def place(buf, res):
        for j in range(buf.shape[0]):
            res[j * own : (j + 1) * own, :] = buf[j].astype(F32)[:own]

    return place


def run_gather_place(p, src, res, buf, place):
    yield from run_gather_ctx(p, src, buf)
    place(buf, res)


def run_reduce_place(p, src, res, land, mid, buf, place):
    yield from run_scatter_dp(p, src, mid, land)
    yield from run_gather_ctx(p, mid, buf)
    place(buf, res)


def run_rows_reduce(p, src, out, land, mid, per):
    yield from run_rows_scatter(p, src, mid, land, per)
    yield from run_gather_ctx(p, mid, out)


def exchange(tasks, n_dp, n_ctx, collective):
    chips = n_ctx // 2
    per = -(-HEADS // n_ctx)
    outs, scratch, counts, runs, copies = [], [], [], [], 0
    for task in tasks:
        kind, array = task[:2]
        shape, more, kept = array.shape, [], array.dtype
        if kind == "gather_ctx":
            shape, run, n = (n_ctx,) + shape, run_gather_ctx, 2 * chips - 1
        elif kind == "scatter_ctx":
            shape, run, n, kept = shape[1:], run_scatter_ctx, 2 * chips - 1, F32
            more = [(chips,) + shape] * 3
        elif kind == "gather_dp":
            shape, run, n = (n_dp,) + shape, run_gather_dp, n_dp - 1
        elif kind == "scatter_dp":
            shape, run, n = shape[1:], run_scatter_dp, n_dp - 1
            more = [(n_dp,) + shape]
        elif kind == "reduce":
            more = [shape, shape[1:]]
            shape, run, n = (n_ctx,) + shape[1:], run_reduce, n_dp - 1 + 2 * chips - 1
        elif kind == "reduce_place":
            more = [shape, shape[1:], (n_ctx,) + shape[1:]]
            shape, n, kept = task[3], n_dp - 1 + 2 * chips - 1, F32
            run = lambda *a, place=task[2]: run_reduce_place(*a, place)
        elif kind == "gather_place":
            more = [(n_ctx,) + shape]
            shape, n, kept = task[3], 2 * chips - 1, F32
            run = lambda *a, place=task[2]: run_gather_place(*a, place)
        elif kind == "rows_reduce":
            more, n = [(n_dp,) + shape, shape], per * (n_dp - 1) + 2 * chips - 1
            shape = (n_ctx,) + shape
            run = lambda *a: run_rows_reduce(*a, per)
        elif kind == "rows_gather":
            width = shape[1]
            shape, n = (per * (width // HEADS), width), per * (n_dp - 1)
            run = lambda *a: run_rows_gather(*a, per)
        outs.append(jax.ShapeDtypeStruct(shape, kept))
        scratch += [pltpu.VMEM(m, array.dtype) for m in more]
        counts.append(len(more))
        runs.append(run)
        copies += n
    kinds = [task[0] for task in tasks]
    use_ctx = any(k not in ("gather_dp", "scatter_dp", "rows_gather") for k in kinds)
    use_dp = any(k not in ("gather_ctx", "scatter_ctx", "gather_place") for k in kinds)

    def kernel(*refs):
        n = len(tasks)
        ins, results, rest = refs[:n], refs[n : 2 * n], list(refs[2 * n :])
        send_sem, recv_sem = rest[-2:]
        p = Places(n_dp, n_ctx, send_sem, recv_sem)
        barrier = pltpu.get_barrier_semaphore()
        partners = []
        if use_ctx:
            partners.append((p.z, p.sibling))
            partners += [(p.z, p.other_chip(d) * 2 + p.core) for d in range(1, chips)]
        if use_dp:
            partners += [(p.other_dp(d), p.me) for d in range(1, n_dp)]
        for partner in partners:
            pl.semaphore_signal(barrier, inc=1, device_id=partner, device_id_type=MESH)
        pl.semaphore_wait(barrier, len(partners))
        live = []
        for i in range(n):
            mine, rest = rest[: counts[i]], rest[counts[i] :]
            live.append(runs[i](p, ins[i], results[i], *mine))
        while live:
            for task in list(live):
                try:
                    next(task)
                except StopIteration:
                    live.remove(task)

    size = lambda shape: 2 * (math.prod(shape[:-1]) + 16) * round_up(shape[-1], 128)
    need = sum(2 * size(task[1].shape) for task in tasks) + sum(2 * size(o.shape) for o in outs)
    need += sum(size(m.shape) for m in scratch)
    sent = sum(size(task[1].shape) for task in tasks)
    vmem = pl.BlockSpec(memory_space=pltpu.VMEM)
    return pl.pallas_call(
        kernel,
        out_shape=outs,
        in_specs=[vmem] * len(tasks),
        out_specs=[vmem] * len(tasks),
        scratch_shapes=scratch
        + [pltpu.SemaphoreType.DMA((copies,)), pltpu.SemaphoreType.DMA((copies,))],
        compiler_params=pltpu.CompilerParams(
            collective_id=collective,
            has_side_effects=True,
            vmem_limit_bytes=min(60 << 20, max(16 << 20, need + need // 4 + (4 << 20))),
        ),
        cost_estimate=pl.CostEstimate(flops=0, bytes_accessed=4 * sent, transcendentals=0),
    )(*[task[1] for task in tasks])


def round_up(n, m):
    return -(-n // m) * m


def make_local(n_dp, n_ctx):
    def local(hidden_in, segment_ids, w_qkv, w_out, w_in, w_down, gain_attn, gain_mlp, cotangent):
        rows, width = hidden_in.shape[1], hidden_in.shape[2]
        head_size = width // HEADS
        scale = head_size ** (-0.5)
        per = -(-HEADS // n_ctx)
        owners = HEADS // per
        tokens = rows * n_ctx
        shard = w_qkv.shape[0]
        hidden_units = w_in.shape[1] // 2
        down_rows = w_down.shape[0]
        own = down_rows // n_ctx
        padded = round_up(own, 16)
        units = n_dp * padded
        cols = per * head_size
        me = lax.axis_index("ctx")
        valid = me < owners
        slot = jnp.minimum(me, owners - 1)

        qkv_mine = lax.dynamic_slice(
            w_qkv.reshape(shard, 3, width), (0, 0, slot * cols), (shard, 3, cols)
        ).reshape(shard, 3 * cols)
        gains = jnp.pad(jnp.stack([gain_attn, gain_mlp]), ((0, 14), (0, 0)))
        in_mine = lax.dynamic_slice(
            w_in.reshape(shard, 2 * n_dp, down_rows), (0, 0, me * own), (shard, 2 * n_dp, own)
        )
        in_mine = jnp.pad(in_mine, ((0, 0), (0, 0), (0, padded - own))).reshape(shard, 2 * units)
        down_mine = jnp.pad(
            lax.dynamic_slice(w_down, (me * own, 0), (own, width)), ((0, padded - own), (0, 0))
        )
        id_row = jnp.pad(segment_ids.astype(BF), ((0, 15), (0, 0)))
        hidden_all, qkv_full, gains_all, id_all, out_full, upstream = exchange(
            [
                ("gather_ctx", hidden_in[0]),
                ("gather_dp", qkv_mine),
                ("gather_dp", gains),
                ("gather_ctx", id_row),
                ("rows_gather", w_out),
                ("gather_ctx", cotangent[0]),
            ],
            n_dp, n_ctx, 0,
        )
        qkv_full = qkv_full.reshape(width, 3 * cols)
        attn_gain = gains_all[:, 0].reshape(1, width).astype(F32)
        mlp_gain = gains_all[:, 1].reshape(1, width).astype(F32)
        source = hidden_all.reshape(tokens, width).astype(F32)
        upstream = upstream.reshape(tokens, width)
        ids = id_all[:, 0].reshape(tokens).astype(jnp.int32)

        cosines, sines = rope_tables(tokens, head_size, per)
        unit_one, inverse_one = normalise(source)
        normed_one = (unit_one * attn_gain).astype(BF)
        projected = dot(normed_one, qkv_full)

        def head_of(part, h):
            start = part * cols + h * head_size
            return projected[:, start : start + head_size]

        queries = jnp.stack([rotary(head_of(0, h), cosines, sines) for h in range(per)]).astype(BF)
        keys = jnp.stack([rotary(head_of(1, h), cosines, sines) for h in range(per)]).astype(BF)
        values = jnp.stack([head_of(2, h) for h in range(per)]).astype(BF)
        chunk = min(tokens, 1024)
        pieces = tokens // chunk
        attention, log_total = [], []
        for c in range(pieces):
            part = slice(c * chunk, (c + 1) * chunk)
            scores = jnp.einsum("hqe,hke->hqk", queries[:, part], keys, preferred_element_type=F32) * scale
            allowed = (ids[part][:, None] == ids[None, :])[None]
            scores = jnp.where(allowed, scores, NEGATIVE)
            highest = jnp.max(scores, axis=-1, keepdims=True)
            weights = jnp.where(allowed, jnp.exp(scores - highest), 0.0)
            total = jnp.sum(weights, axis=-1, keepdims=True)
            summed = jnp.einsum("hqk,hke->hqe", weights.astype(BF), values, preferred_element_type=F32)
            attention.append(summed / total)
            log_total.append(highest + jnp.log(total))
        attention_all = jnp.concatenate(attention, axis=1)
        attention_all = jnp.where(valid, attention_all, 0.0)
        attended = jnp.concatenate([attention_all[h] for h in range(per)], axis=1).astype(BF)
        branch, in_full = exchange(
            [
                ("scatter_ctx", dot(attended, out_full).astype(BF).reshape(n_ctx, rows, width)),
                ("gather_dp", in_mine),
            ],
            n_dp, n_ctx, 1,
        )
        in_full = in_full.reshape(width, 2 * units)
        middle = hidden_in[0].astype(F32) + branch
        unit_two, inverse_two = normalise(middle)
        normed_two, down_full = exchange(
            [("gather_ctx", (unit_two * mlp_gain).astype(BF)), ("gather_dp", down_mine)],
            n_dp, n_ctx, 2,
        )
        normed_two = normed_two.reshape(tokens, width)
        down_full = down_full.reshape(units, width)
        lifted = dot(normed_two, in_full)
        gate_in, gate_up = lifted[:, :units], lifted[:, units:]
        mixed_value, pull_gate = jax.vjp(geglu, gate_in, gate_up)
        mixed_units = mixed_value.astype(BF)
        out_part = dot(mixed_units, down_full).astype(BF)
        grad_gate_in, grad_gate_up = pull_gate(dot_t(upstream, down_full))
        grad_lifted = jnp.concatenate([grad_gate_in, grad_gate_up], axis=1).astype(BF)
        grad_normed_part = dot_t(grad_lifted, in_full).astype(BF)
        grad_in = t_dot(normed_two, grad_lifted).astype(BF).reshape(n_dp, shard, 2 * units)
        grad_down = t_dot(mixed_units, upstream).astype(BF).reshape(n_dp, padded, width)
        grad_normed_two, out_sum, grad_in = exchange(
            [
                ("scatter_ctx", grad_normed_part.reshape(n_ctx, rows, width)),
                ("scatter_ctx", out_part.reshape(n_ctx, rows, width)),
                ("scatter_dp", grad_in),
            ],
            n_dp, n_ctx, 3,
        )
        result = (middle + out_sum).astype(BF)
        gain_part = jnp.sum(grad_normed_two * unit_two, axis=0, keepdims=True)
        grad_middle = cotangent[0].astype(F32) + normalise_back(
            unit_two, inverse_two, grad_normed_two * mlp_gain
        )
        gain_rows = jnp.pad(gain_part.astype(BF), ((0, 15), (0, 0)))
        grad_branch, gain_rows, grad_down = exchange(
            [
                ("gather_ctx", grad_middle.astype(BF)),
                ("gather_ctx", gain_rows),
                ("scatter_dp", grad_down),
            ],
            n_dp, n_ctx, 4,
        )
        grad_branch = grad_branch.reshape(tokens, width)
        mlp_gain_sum = jnp.sum(gain_rows[:, 0].astype(F32), axis=0)
        grad_attended = dot_t(grad_branch, out_full)
        grad_heads = jnp.stack(
            [grad_attended[:, h * head_size : (h + 1) * head_size] for h in range(per)]
        ).astype(BF)
        grad_out = t_dot(attended, grad_branch).astype(BF)
        grad_queries, grad_keys, grad_values = [], 0.0, 0.0
        for c in range(pieces):
            part = slice(c * chunk, (c + 1) * chunk)
            scores = jnp.einsum("hqe,hke->hqk", queries[:, part], keys, preferred_element_type=F32) * scale
            allowed = (ids[part][:, None] == ids[None, :])[None]
            probs = jnp.where(allowed, jnp.exp(scores - log_total[c]), 0.0)
            grad_part = grad_heads[:, part]
            products = jnp.sum(grad_part.astype(F32) * attention_all[:, part], axis=-1, keepdims=True)
            grad_probs = jnp.einsum("hqe,hke->hqk", grad_part, values, preferred_element_type=F32)
            grad_scores = (probs * (grad_probs - products)).astype(BF)
            grad_queries.append(
                scale * jnp.einsum("hqk,hke->hqe", grad_scores, keys, preferred_element_type=F32)
            )
            grad_keys += scale * jnp.einsum(
                "hqk,hqe->hke", grad_scores, queries[:, part], preferred_element_type=F32
            )
            grad_values += jnp.einsum(
                "hqk,hqe->hke", probs.astype(BF), grad_part, preferred_element_type=F32
            )
        grad_queries = jnp.concatenate(grad_queries, axis=1)
        grad_projected = jnp.concatenate(
            [rotary_back(grad_queries[h], cosines, sines) for h in range(per)]
            + [rotary_back(grad_keys[h], cosines, sines) for h in range(per)]
            + [grad_values[h] for h in range(per)],
            axis=1,
        )
        grad_projected = jnp.where(valid, grad_projected, 0.0).astype(BF)
        grad_normed_one = dot_t(grad_projected, qkv_full)
        attn_gain_part = jnp.sum(grad_normed_one * unit_one, axis=0)
        grad_qkv = t_dot(normed_one, grad_projected).astype(BF).reshape(n_dp, shard, 3 * cols)
        gain_sums = jnp.stack([attn_gain_part, mlp_gain_sum]).astype(BF).reshape(2, n_dp, shard)
        gain_sums = jnp.pad(jnp.transpose(gain_sums, (1, 0, 2)), ((0, 0), (0, 14), (0, 0)))

        def place_heads(buf, res):
            for j in range(owners):
                block = buf[j].astype(F32)
                for part in range(3):
                    start = part * width + j * cols
                    res[:, start : start + cols] = block[:, part * cols : (part + 1) * cols]

        back, share_in, share_qkv, out_all, gains_last, share_down = exchange(
            [
                ("scatter_ctx", grad_normed_one.astype(BF).reshape(n_ctx, rows, width)),
                ("gather_place", grad_in, place_columns(2 * n_dp, own), (shard, 2 * hidden_units)),
                ("reduce_place", grad_qkv, place_heads, (shard, 3 * width)),
                ("rows_reduce", grad_out),
                ("reduce", gain_sums),
                ("gather_place", grad_down, place_rows(own), (down_rows, width)),
            ],
            n_dp, n_ctx, 5,
        )
        unit_own, inverse_own = normalise(hidden_in[0].astype(F32))
        grad_input = grad_middle + normalise_back(unit_own, inverse_own, back * attn_gain)

        share_attn = jnp.sum(gains_last[:, 0].astype(F32), axis=0)
        share_mlp = gains_last[0, 1].astype(F32)
        out_rows = width // n_dp
        share_out = lax.dynamic_slice(
            out_all.reshape(n_ctx * cols, width), (lax.axis_index("dp") * out_rows, 0), (out_rows, width)
        ).astype(F32)
        return (
            result[None],
            grad_input[None],
            share_qkv,
            share_out,
            share_in,
            share_down,
            share_attn,
            share_mlp,
        )

    return local


def solution(mesh):
    tokens = P("dp", "ctx", None)
    weight = P("dp", None)
    in_specs = (tokens, P("dp", "ctx")) + (weight,) * 4 + (P("dp"), P("dp"), tokens)
    out_specs = (tokens, tokens) + (weight,) * 4 + (P("dp"), P("dp"))
    return jax.shard_map(
        make_local(mesh.shape["dp"], mesh.shape["ctx"]),
        mesh=mesh,
        in_specs=in_specs,
        out_specs=out_specs,
        check_vma=False,
    )
```

```python
import math

import jax
import jax.numpy as jnp
import numpy as np
from jax import lax
from jax.experimental import pallas as pl
from jax.experimental.pallas import tpu as pltpu
from jax.sharding import PartitionSpec as P

HEADS = 12
EPSILON = 1e-05
ROPE_THETA = 160000.0
NEGATIVE = -1e30
F32 = jnp.float32
BF = jnp.bfloat16


def dot(a, b):
    return jnp.dot(a, b, preferred_element_type=F32)


def dot_t(a, b):
    return lax.dot_general(a, b, (((1,), (1,)), ((), ())), preferred_element_type=F32)


def t_dot(a, b):
    return lax.dot_general(a, b, (((0,), (0,)), ((), ())), preferred_element_type=F32)


def normalise(values):
    average = jnp.mean(values, axis=-1, keepdims=True)
    centred = values - average
    spread = jnp.mean(centred * centred, axis=-1, keepdims=True)
    inverse = lax.rsqrt(spread + EPSILON)
    return centred * inverse, inverse


def normalise_back(unit, inverse, grad):
    mean_grad = jnp.mean(grad, axis=-1, keepdims=True)
    mean_both = jnp.mean(grad * unit, axis=-1, keepdims=True)
    return inverse * (grad - mean_grad - unit * mean_both)


def rope_tables(row_count, head_size, heads):
    position = np.arange(row_count).astype(np.float32)
    power = -np.arange(0, head_size, 2).astype(np.float32) / np.float32(head_size)
    frequency = (ROPE_THETA ** power.astype(np.float64)).astype(np.float32)
    angles = position[:, None] * frequency[None, :]
    angles = np.concatenate([angles, angles], axis=-1).astype(np.float64)
    return np.cos(angles).astype(np.float32), np.sin(angles).astype(np.float32)


def rotary(values, cosines, sines):
    half = values.shape[-1] // 2
    turned = jnp.concatenate([-values[..., half:], values[..., :half]], axis=-1)
    return values * cosines + turned * sines


def rotary_back(grads, cosines, sines):
    half = grads.shape[-1] // 2
    shifted = grads * sines
    return grads * cosines + jnp.concatenate([shifted[..., half:], -shifted[..., :half]], axis=-1)


def geglu(gate_in, gate_up):
    return jax.nn.gelu(gate_in, approximate=False) * gate_up


MESH = pl.DeviceIdType.MESH


class Places:
    def __init__(self, n_dp, n_ctx, send_sem, recv_sem):
        self.n_dp, self.n_ctx, self.chips = n_dp, n_ctx, n_ctx // 2
        self.z = lax.axis_index("dp")
        self.me = lax.axis_index("ctx")
        self.chip, self.core = self.me // 2, self.me % 2
        self.sibling = self.chip * 2 + 1 - self.core
        self.send_sem, self.recv_sem, self.used = send_sem, recv_sem, 0

    def other_chip(self, d):
        return jnp.bitwise_xor(self.chip, d)

    def other_dp(self, d):
        return jnp.bitwise_xor(self.z, d)

    def copy(self, src, dst, z, ctx):
        k = self.used
        self.used += 1
        return pltpu.make_async_remote_copy(
            src_ref=src,
            dst_ref=dst,
            send_sem=self.send_sem.at[k],
            recv_sem=self.recv_sem.at[k],
            device_id=(z, ctx),
            device_id_type=MESH,
        )


def run_gather_ctx(p, src, out):
    first, second = [], []
    for d in range(1, p.chips):
        peer = p.other_chip(d) * 2 + p.core
        first.append(p.copy(src, out.at[p.me], p.z, peer))
        first[-1].start()
    near = p.copy(src, out.at[p.me], p.z, p.sibling)
    near.start()
    out[p.me] = src[...]
    yield
    for d in range(1, p.chips):
        first[d - 1].wait_recv()
        held = out.at[p.other_chip(d) * 2 + p.core]
        second.append(p.copy(held, held, p.z, p.sibling))
        second[-1].start()
        yield
    for item in first:
        item.wait_send()
    near.wait()
    for item in second:
        item.wait()


def run_scatter_ctx(p, src, out, sib, acc, land):
    near, far = [], []
    for d in list(range(1, p.chips)) + [0]:
        chip = p.other_chip(d)
        near.append(p.copy(src.at[chip * 2 + 1 - p.core], sib.at[d], p.z, p.sibling))
        near[-1].start()
    yield
    for d in range(1, p.chips):
        near[d - 1].wait_recv()
        chip = p.other_chip(d)
        acc[d] = (src[chip * 2 + p.core].astype(F32) + sib[d].astype(F32)).astype(acc.dtype)
        far.append(p.copy(acc.at[d], land.at[d], p.z, chip * 2 + p.core))
        far[-1].start()
    near[-1].wait_recv()
    out[...] = src[p.me].astype(F32) + sib[0].astype(F32)
    yield
    for d in range(1, p.chips):
        far[d - 1].wait_recv()
        out[...] += land[d].astype(F32)
    for item in far + near:
        item.wait_send()


def run_gather_dp(p, src, out):
    copies = []
    for d in range(1, p.n_dp):
        copies.append(p.copy(src, out.at[p.z], p.other_dp(d), p.me))
        copies[-1].start()
    out[p.z] = src[...]
    yield
    for item in copies:
        item.wait()


def run_scatter_dp(p, src, out, land):
    copies = []
    for d in range(1, p.n_dp):
        copies.append(p.copy(src.at[p.other_dp(d)], land.at[d], p.other_dp(d), p.me))
        copies[-1].start()
    yield
    total = src[p.z].astype(F32)
    for d in range(1, p.n_dp):
        copies[d - 1].wait_recv()
        total = total + land[d].astype(F32)
    out[...] = total.astype(out.dtype)
    for item in copies:
        item.wait_send()


def run_reduce(p, src, out, land, mid):
    yield from run_scatter_dp(p, src, mid, land)
    yield from run_gather_ctx(p, mid, out)


def head_place(p, s, per):
    owners = HEADS // per
    head = jnp.minimum(p.me, owners - 1) * per + s
    each = HEADS // p.n_dp
    return head // each, head % each


def run_rows_gather(p, src, out, per):
    size = out.shape[0] // per
    jobs = []
    for s in range(per):
        owner, place = head_place(p, s, per)
        rows = src.at[pl.ds(pl.multiple_of(place * size, size), size)]
        slot = out.at[pl.ds(s * size, size)]
        copies = [p.copy(rows, slot, p.other_dp(d), p.me) for d in range(1, p.n_dp)]
        jobs.append((owner, copies))

        @pl.when(p.z == owner)
        def _():
            for item in copies:
                item.start()
            out[pl.ds(s * size, size)] = src[pl.ds(pl.multiple_of(place * size, size), size)]

    yield
    for owner, copies in jobs:
        for d in range(1, p.n_dp):
            item = copies[d - 1]

            @pl.when(p.z == owner)
            def _():
                item.wait_send()

            @pl.when(p.other_dp(d) == owner)
            def _():
                item.wait_recv()


def run_rows_scatter(p, src, out, land, per):
    size = src.shape[0] // per
    jobs = []
    for s in range(per):
        owner, _ = head_place(p, s, per)
        slot = pl.ds(s * size, size)
        copies = [
            p.copy(src.at[slot], land.at[d, slot], p.other_dp(d), p.me) for d in range(1, p.n_dp)
        ]
        jobs.append((owner, slot, copies))
        for d in range(1, p.n_dp):
            item = copies[d - 1]

            @pl.when(p.other_dp(d) == owner)
            def _():
                item.start()

    yield
    for owner, slot, copies in jobs:

        @pl.when(p.z == owner)
        def _():
            total = src[slot].astype(F32)
            for d in range(1, p.n_dp):
                copies[d - 1].wait_recv()
                total = total + land[d, slot].astype(F32)
            out[slot] = total.astype(out.dtype)

        @pl.when(p.z != owner)
        def _():
            out[slot] = src[slot]

        for d in range(1, p.n_dp):
            item = copies[d - 1]

            @pl.when(p.other_dp(d) == owner)
            def _():
                item.wait_send()


def place_columns(parts, own):
    def place(buf, res):
        n, width = buf.shape[0], buf.shape[2] // parts
        for j in range(n):
            block = buf[j].astype(F32)
            for p in range(parts):
                res[:, (p * n + j) * own : (p * n + j + 1) * own] = block[:, p * width : p * width + own]

    return place


def place_rows(own):
    def place(buf, res):
        for j in range(buf.shape[0]):
            res[j * own : (j + 1) * own, :] = buf[j].astype(F32)[:own]

    return place


def run_gather_place(p, src, res, buf, place):
    yield from run_gather_ctx(p, src, buf)
    place(buf, res)


def run_reduce_place(p, src, res, land, mid, buf, place):
    yield from run_scatter_dp(p, src, mid, land)
    yield from run_gather_ctx(p, mid, buf)
    place(buf, res)


def run_rows_reduce(p, src, out, land, mid, per):
    yield from run_rows_scatter(p, src, mid, land, per)
    yield from run_gather_ctx(p, mid, out)


def exchange(tasks, n_dp, n_ctx, collective):
    chips = n_ctx // 2
    per = -(-HEADS // n_ctx)
    outs, scratch, counts, runs, copies = [], [], [], [], 0
    for task in tasks:
        kind, array = task[:2]
        shape, more, kept = array.shape, [], array.dtype
        if kind == "gather_ctx":
            shape, run, n = (n_ctx,) + shape, run_gather_ctx, 2 * chips - 1
        elif kind == "scatter_ctx":
            shape, run, n, kept = shape[1:], run_scatter_ctx, 2 * chips - 1, F32
            more = [(chips,) + shape] * 3
        elif kind == "gather_dp":
            shape, run, n = (n_dp,) + shape, run_gather_dp, n_dp - 1
        elif kind == "scatter_dp":
            shape, run, n = shape[1:], run_scatter_dp, n_dp - 1
            more = [(n_dp,) + shape]
        elif kind == "reduce":
            more = [shape, shape[1:]]
            shape, run, n = (n_ctx,) + shape[1:], run_reduce, n_dp - 1 + 2 * chips - 1
        elif kind == "reduce_place":
            more = [shape, shape[1:], (n_ctx,) + shape[1:]]
            shape, n, kept = task[3], n_dp - 1 + 2 * chips - 1, F32
            run = lambda *a, place=task[2]: run_reduce_place(*a, place)
        elif kind == "gather_place":
            more = [(n_ctx,) + shape]
            shape, n, kept = task[3], 2 * chips - 1, F32
            run = lambda *a, place=task[2]: run_gather_place(*a, place)
        elif kind == "rows_reduce":
            more, n = [(n_dp,) + shape, shape], per * (n_dp - 1) + 2 * chips - 1
            shape = (n_ctx,) + shape
            run = lambda *a: run_rows_reduce(*a, per)
        elif kind == "rows_gather":
            width = shape[1]
            shape, n = (per * (width // HEADS), width), per * (n_dp - 1)
            run = lambda *a: run_rows_gather(*a, per)
        outs.append(jax.ShapeDtypeStruct(shape, kept))
        scratch += [pltpu.VMEM(m, array.dtype) for m in more]
        counts.append(len(more))
        runs.append(run)
        copies += n
    kinds = [task[0] for task in tasks]
    use_ctx = any(k not in ("gather_dp", "scatter_dp", "rows_gather") for k in kinds)
    use_dp = any(k not in ("gather_ctx", "scatter_ctx", "gather_place") for k in kinds)

    def kernel(*refs):
        n = len(tasks)
        ins, results, rest = refs[:n], refs[n : 2 * n], list(refs[2 * n :])
        send_sem, recv_sem = rest[-2:]
        p = Places(n_dp, n_ctx, send_sem, recv_sem)
        barrier = pltpu.get_barrier_semaphore()
        partners = []
        if use_ctx:
            partners.append((p.z, p.sibling))
            partners += [(p.z, p.other_chip(d) * 2 + p.core) for d in range(1, chips)]
        if use_dp:
            partners += [(p.other_dp(d), p.me) for d in range(1, n_dp)]
        for partner in partners:
            pl.semaphore_signal(barrier, inc=1, device_id=partner, device_id_type=MESH)
        pl.semaphore_wait(barrier, len(partners))
        live = []
        for i in range(n):
            mine, rest = rest[: counts[i]], rest[counts[i] :]
            live.append(runs[i](p, ins[i], results[i], *mine))
        while live:
            for task in list(live):
                try:
                    next(task)
                except StopIteration:
                    live.remove(task)

    size = lambda shape: 2 * (math.prod(shape[:-1]) + 16) * round_up(shape[-1], 128)
    need = sum(2 * size(task[1].shape) for task in tasks) + sum(2 * size(o.shape) for o in outs)
    need += sum(size(m.shape) for m in scratch)
    sent = sum(size(task[1].shape) for task in tasks)
    vmem = pl.BlockSpec(memory_space=pltpu.VMEM)
    return pl.pallas_call(
        kernel,
        out_shape=outs,
        in_specs=[vmem] * len(tasks),
        out_specs=[vmem] * len(tasks),
        scratch_shapes=scratch
        + [pltpu.SemaphoreType.DMA((copies,)), pltpu.SemaphoreType.DMA((copies,))],
        compiler_params=pltpu.CompilerParams(
            collective_id=collective,
            has_side_effects=True,
            vmem_limit_bytes=min(60 << 20, max(16 << 20, need + need // 4 + (4 << 20))),
        ),
        cost_estimate=pl.CostEstimate(flops=0, bytes_accessed=4 * sent, transcendentals=0),
    )(*[task[1] for task in tasks])


def round_up(n, m):
    return -(-n // m) * m


def make_local(n_dp, n_ctx):
    def local(hidden_in, segment_ids, w_qkv, w_out, w_in, w_down, gain_attn, gain_mlp, cotangent):
        rows, width = hidden_in.shape[1], hidden_in.shape[2]
        head_size = width // HEADS
        scale = head_size ** (-0.5)
        per = -(-HEADS // n_ctx)
        owners = HEADS // per
        tokens = rows * n_ctx
        shard = w_qkv.shape[0]
        hidden_units = w_in.shape[1] // 2
        down_rows = w_down.shape[0]
        own = down_rows // n_ctx
        padded = round_up(own, 16)
        units = n_dp * padded
        cols = per * head_size
        me = lax.axis_index("ctx")
        valid = me < owners
        slot = jnp.minimum(me, owners - 1)

        qkv_mine = lax.dynamic_slice(
            w_qkv.reshape(shard, 3, width), (0, 0, slot * cols), (shard, 3, cols)
        ).reshape(shard, 3 * cols)
        gains = jnp.pad(jnp.stack([gain_attn, gain_mlp]), ((0, 14), (0, 0)))
        in_mine = lax.dynamic_slice(
            w_in.reshape(shard, 2 * n_dp, down_rows), (0, 0, me * own), (shard, 2 * n_dp, own)
        )
        in_mine = jnp.pad(in_mine, ((0, 0), (0, 0), (0, padded - own))).reshape(shard, 2 * units)
        down_mine = jnp.pad(
            lax.dynamic_slice(w_down, (me * own, 0), (own, width)), ((0, padded - own), (0, 0))
        )
        id_row = jnp.pad(segment_ids.astype(BF), ((0, 15), (0, 0)))
        hidden_all, qkv_full, gains_all, id_all, out_full, upstream = exchange(
            [
                ("gather_ctx", hidden_in[0]),
                ("gather_dp", qkv_mine),
                ("gather_dp", gains),
                ("gather_ctx", id_row),
                ("rows_gather", w_out),
                ("gather_ctx", cotangent[0]),
            ],
            n_dp, n_ctx, 0,
        )
        qkv_full = qkv_full.reshape(width, 3 * cols)
        attn_gain = gains_all[:, 0].reshape(1, width).astype(F32)
        mlp_gain = gains_all[:, 1].reshape(1, width).astype(F32)
        source = hidden_all.reshape(tokens, width).astype(F32)
        upstream = upstream.reshape(tokens, width)
        ids = id_all[:, 0].reshape(tokens).astype(jnp.int32)

        cosines, sines = rope_tables(tokens, head_size, per)
        unit_one, inverse_one = normalise(source)
        normed_one = (unit_one * attn_gain).astype(BF)
        projected = dot(normed_one, qkv_full)

        def head_of(part, h):
            start = part * cols + h * head_size
            return projected[:, start : start + head_size]

        queries = jnp.stack([rotary(head_of(0, h), cosines, sines) for h in range(per)]).astype(BF)
        keys = jnp.stack([rotary(head_of(1, h), cosines, sines) for h in range(per)]).astype(BF)
        values = jnp.stack([head_of(2, h) for h in range(per)]).astype(BF)
        chunk = min(tokens, 1024)
        pieces = tokens // chunk
        attention, kept, inverses = [], [], []
        for c in range(pieces):
            part = slice(c * chunk, (c + 1) * chunk)
            scores = jnp.einsum("hqe,hke->hqk", queries[:, part], keys, preferred_element_type=F32) * scale
            allowed = (ids[part][:, None] == ids[None, :])[None]
            scores = jnp.where(allowed, scores, NEGATIVE)
            highest = jnp.max(scores, axis=-1, keepdims=True)
            weights = jnp.where(allowed, jnp.exp(scores - highest), 0.0)
            total = jnp.sum(weights, axis=-1, keepdims=True)
            kept.append(weights.astype(BF))
            inverses.append(1.0 / total)
            summed = jnp.einsum("hqk,hke->hqe", kept[c], values, preferred_element_type=F32)
            attention.append(summed * inverses[c])
        attention_all = jnp.concatenate(attention, axis=1)
        attention_all = jnp.where(valid, attention_all, 0.0)
        attended = jnp.concatenate([attention_all[h] for h in range(per)], axis=1).astype(BF)
        branch, in_full = exchange(
            [
                ("scatter_ctx", dot(attended, out_full).astype(BF).reshape(n_ctx, rows, width)),
                ("gather_dp", in_mine),
            ],
            n_dp, n_ctx, 1,
        )
        in_full = in_full.reshape(width, 2 * units)
        middle = hidden_in[0].astype(F32) + branch
        unit_two, inverse_two = normalise(middle)
        normed_two, down_full = exchange(
            [("gather_ctx", (unit_two * mlp_gain).astype(BF)), ("gather_dp", down_mine)],
            n_dp, n_ctx, 2,
        )
        normed_two = normed_two.reshape(tokens, width)
        down_full = down_full.reshape(units, width)
        lifted = dot(normed_two, in_full)
        gate_in, gate_up = lifted[:, :units], lifted[:, units:]
        mixed_value, pull_gate = jax.vjp(geglu, gate_in, gate_up)
        mixed_units = mixed_value.astype(BF)
        out_part = dot(mixed_units, down_full).astype(BF)
        grad_gate_in, grad_gate_up = pull_gate(dot_t(upstream, down_full))
        grad_lifted = jnp.concatenate([grad_gate_in, grad_gate_up], axis=1).astype(BF)
        grad_normed_part = dot_t(grad_lifted, in_full).astype(BF)
        grad_in = t_dot(normed_two, grad_lifted).astype(BF).reshape(n_dp, shard, 2 * units)
        grad_down = t_dot(mixed_units, upstream).astype(BF).reshape(n_dp, padded, width)
        grad_normed_two, out_sum, grad_in = exchange(
            [
                ("scatter_ctx", grad_normed_part.reshape(n_ctx, rows, width)),
                ("scatter_ctx", out_part.reshape(n_ctx, rows, width)),
                ("scatter_dp", grad_in),
            ],
            n_dp, n_ctx, 3,
        )
        result = (middle + out_sum).astype(BF)
        gain_part = jnp.sum(grad_normed_two * unit_two, axis=0, keepdims=True)
        grad_middle = cotangent[0].astype(F32) + normalise_back(
            unit_two, inverse_two, grad_normed_two * mlp_gain
        )
        gain_rows = jnp.pad(gain_part.astype(BF), ((0, 15), (0, 0)))
        grad_branch, gain_rows, grad_down = exchange(
            [
                ("gather_ctx", grad_middle.astype(BF)),
                ("gather_ctx", gain_rows),
                ("scatter_dp", grad_down),
            ],
            n_dp, n_ctx, 4,
        )
        grad_branch = grad_branch.reshape(tokens, width)
        mlp_gain_sum = jnp.sum(gain_rows[:, 0].astype(F32), axis=0)
        grad_attended = dot_t(grad_branch, out_full)
        grad_heads = jnp.stack(
            [grad_attended[:, h * head_size : (h + 1) * head_size] for h in range(per)]
        ).astype(BF)
        grad_out = t_dot(attended, grad_branch).astype(BF)
        grad_queries, grad_keys, grad_values = [], 0.0, 0.0
        for c in range(pieces):
            part = slice(c * chunk, (c + 1) * chunk)
            grad_part = grad_heads[:, part]
            products = jnp.sum(grad_part.astype(F32) * attention_all[:, part], axis=-1, keepdims=True)
            grad_probs = jnp.einsum("hqe,hke->hqk", grad_part, values, preferred_element_type=F32)
            grad_scores = (kept[c].astype(F32) * ((grad_probs - products) * inverses[c])).astype(BF)
            grad_queries.append(
                scale * jnp.einsum("hqk,hke->hqe", grad_scores, keys, preferred_element_type=F32)
            )
            grad_keys += scale * jnp.einsum(
                "hqk,hqe->hke", grad_scores, queries[:, part], preferred_element_type=F32
            )
            grad_values += jnp.einsum(
                "hqk,hqe->hke",
                kept[c],
                (grad_part.astype(F32) * inverses[c]).astype(BF),
                preferred_element_type=F32,
            )
        grad_queries = jnp.concatenate(grad_queries, axis=1)
        grad_projected = jnp.concatenate(
            [rotary_back(grad_queries[h], cosines, sines) for h in range(per)]
            + [rotary_back(grad_keys[h], cosines, sines) for h in range(per)]
            + [grad_values[h] for h in range(per)],
            axis=1,
        )
        grad_projected = jnp.where(valid, grad_projected, 0.0).astype(BF)
        grad_normed_one = dot_t(grad_projected, qkv_full)
        attn_gain_part = jnp.sum(grad_normed_one * unit_one, axis=0)
        grad_qkv = t_dot(normed_one, grad_projected).astype(BF).reshape(n_dp, shard, 3 * cols)
        gain_sums = jnp.stack([attn_gain_part, mlp_gain_sum]).astype(BF).reshape(2, n_dp, shard)
        gain_sums = jnp.pad(jnp.transpose(gain_sums, (1, 0, 2)), ((0, 0), (0, 14), (0, 0)))

        def place_heads(buf, res):
            for j in range(owners):
                block = buf[j].astype(F32)
                for part in range(3):
                    start = part * width + j * cols
                    res[:, start : start + cols] = block[:, part * cols : (part + 1) * cols]

        back, share_in, share_qkv, out_all, gains_last, share_down = exchange(
            [
                ("scatter_ctx", grad_normed_one.astype(BF).reshape(n_ctx, rows, width)),
                ("gather_place", grad_in, place_columns(2 * n_dp, own), (shard, 2 * hidden_units)),
                ("reduce_place", grad_qkv, place_heads, (shard, 3 * width)),
                ("rows_reduce", grad_out),
                ("reduce", gain_sums),
                ("gather_place", grad_down, place_rows(own), (down_rows, width)),
            ],
            n_dp, n_ctx, 5,
        )
        unit_own, inverse_own = normalise(hidden_in[0].astype(F32))
        grad_input = grad_middle + normalise_back(unit_own, inverse_own, back * attn_gain)

        share_attn = jnp.sum(gains_last[:, 0].astype(F32), axis=0)
        share_mlp = gains_last[0, 1].astype(F32)
        out_rows = width // n_dp
        share_out = lax.dynamic_slice(
            out_all.reshape(n_ctx * cols, width), (lax.axis_index("dp") * out_rows, 0), (out_rows, width)
        ).astype(F32)
        return (
            result[None],
            grad_input[None],
            share_qkv,
            share_out,
            share_in,
            share_down,
            share_attn,
            share_mlp,
        )

    return local


def solution(mesh):
    tokens = P("dp", "ctx", None)
    weight = P("dp", None)
    in_specs = (tokens, P("dp", "ctx")) + (weight,) * 4 + (P("dp"), P("dp"), tokens)
    out_specs = (tokens, tokens) + (weight,) * 4 + (P("dp"), P("dp"))
    return jax.shard_map(
        make_local(mesh.shape["dp"], mesh.shape["ctx"]),
        mesh=mesh,
        in_specs=in_specs,
        out_specs=out_specs,
        check_vma=False,
    )
```
